32 devices in a mesh: section: 4 (over z), ctx: 8 (over y, x, core).
Axes of the slice: x: 2, y: 2, z: 4, core: 2. Of those that a mesh axis runs over, the one named last changes fastest.
Arguments:
- queries: bfloat16 [4, 2048, 2560], P('section', 'ctx'), may hold values from -5 to 5
- keys: bfloat16 [4, 2048, 512], P('section', 'ctx'), may hold values from -5 to 5
- values: bfloat16 [4, 2048, 512], P('section', 'ctx'), may hold values from -6 to 6
- output_cotangent: bfloat16 [4, 2048, 2560], P('section', 'ctx'), may hold values from -6 to 6
- doc_start: int32 [4, 2048], P('section', 'ctx'), may hold values from 0 to 2047, as said below
Outputs:
- attn: bfloat16 [4, 2048, 2560], P('section', 'ctx')
- handed_dq: bfloat16 [4, 2048, 2560], P('section', 'ctx')
- handed_kv: bfloat16 [4, 2, 2048, 512], P('section', None, 'ctx')
The draws below stay inside these ranges and needn't reach their ends.
Inputs may be any that keep to these rules, and one draw needn't show every extreme that they name: doc_start[m, i] is the first position of the document holding token i; documents are 768 tokens long at most, every microbatch holds one of exactly 768 tokens, and its last token is a document of its own.
All inputs are finite; a program needn't handle non-finite values.
Results may differ from the reference program's by a relative error of at most 0.012.
The reference program's roundings to bfloat16 on the way (of `prob_b`, `dscore` and `grad_q`) count: a program that leaves them out, or rounds other values in their place, can miss the bound.
Values may be sent and summed in bfloat16 or wider, within the bound.
A program may use at most 64 MiB of HBM per device.

```python
import jax
import jax.numpy as jnp
from jax import lax

QUERY_HEADS = 20
KEY_VALUE_HEADS = 4
HEAD_WIDTH = 128
REACH = 3
TOK_DEV = 256
QUERY_PER_KV = 5
TOKEN_LENGTH = 2048
MICROBATCH_COUNT = 4
MOST = 768
N_CTX = 8


def drawn_pair(key):
    base = jax.random.fold_in(key, 1234)
    key_q, key_k = jax.random.split(base, 2)
    query_shape = (MICROBATCH_COUNT, TOKEN_LENGTH, QUERY_HEADS * HEAD_WIDTH)
    key_shape = (MICROBATCH_COUNT, TOKEN_LENGTH, KEY_VALUE_HEADS * HEAD_WIDTH)
    queries_out = jnp.clip(jax.random.normal(key_q, query_shape, jnp.float32), -4.0, 4.0)
    keys_out = jnp.clip(jax.random.normal(key_k, key_shape, jnp.float32), -4.0, 4.0)
    return (queries_out, keys_out)


def draw_queries(key, part):
    return drawn_pair(key)[0].astype(jnp.bfloat16)


def draw_keys(key, part):
    return drawn_pair(key)[1].astype(jnp.bfloat16)


def draw_doc_start(key, part):
    base = jax.random.fold_in(key, 99)
    keys_all = jax.random.split(base, MICROBATCH_COUNT)
    lower = max(1, MOST // 64)
    upper = max(lower + 1, MOST // 8)

    def single(subkey):
        key_a, key_b, key_c = jax.random.split(subkey, 3)
        short = jax.random.randint(key_a, (TOKEN_LENGTH,), lower, upper)
        longer = jax.random.randint(key_b, (TOKEN_LENGTH,), upper, MOST + 1)
        chosen = jax.random.randint(key_c, (TOKEN_LENGTH,), 0, 4) == 0
        lengths = jnp.where(chosen, longer, short)
        lengths = lengths.at[0].set(short[0]).at[1].set(MOST)
        ends = jnp.cumsum(lengths).astype(jnp.int32)
        rows = jnp.arange(TOKEN_LENGTH, dtype=jnp.int32)
        index = jnp.searchsorted(ends, rows, side='right')
        begins = jnp.concatenate([jnp.zeros((1,), jnp.int32), ends[:-1]])
        result = begins[index].astype(jnp.int32)
        return result.at[TOKEN_LENGTH - 1].set(TOKEN_LENGTH - 1)
    return jax.vmap(single)(keys_all)


def level_of(own_key, shape, cuts, least, high):
    factor_of, own = 1.0, jax.random.fold_in(own_key, 6)
    for dim, blocks in cuts:
        draws = jnp.exp(jax.random.uniform(jax.random.fold_in(own, dim), (blocks,), jnp.float32, least / len(cuts), high / len(cuts)))
        factor_of = factor_of * jnp.repeat(draws, shape[dim] // blocks).reshape([-1 if axis == dim else 1 for axis in range(len(shape))])
    return factor_of


def centred(stream_key, shape, width, limit, pieces=(), kind=jnp.bfloat16):
    array = width * jax.random.normal(stream_key, shape, jnp.float32)
    if pieces:
        array = array * level_of(stream_key, shape, pieces, -0.22, 0.18)
    return jnp.clip(array, -limit, limit).astype(kind)


def setup_inputs(seed: int = 0) -> dict:
    seeds = jax.random.split(jax.random.key(seed), 6)
    return {
        "queries": draw_queries(jax.random.fold_in(seeds[5], 71), 0),
        "keys": draw_keys(jax.random.fold_in(seeds[5], 71), 0),
        "values": centred(seeds[2], (MICROBATCH_COUNT, TOKEN_LENGTH, KEY_VALUE_HEADS * HEAD_WIDTH), 1.0, 6.0, ((0, 4), (1, 8))),
        "output_cotangent": centred(seeds[3], (MICROBATCH_COUNT, TOKEN_LENGTH, QUERY_HEADS * HEAD_WIDTH), 1.0, 6.0, ((0, 4), (1, 8))),
        "doc_start": draw_doc_start(jax.random.fold_in(seeds[5], 71), 0),
    }


def group_terms(query_part, dout_part, key_part, value_part, visible, scale):
    query_f = query_part.astype(jnp.float32)
    dout_f = dout_part.astype(jnp.float32)
    key_f = key_part.astype(jnp.float32)
    value_f = value_part.astype(jnp.float32)
    scores = jnp.einsum("tgd,wd->gtw", query_f, key_f) * scale
    scores = jnp.where(visible[None], scores, -jnp.inf)
    top = jnp.max(scores, axis=-1, keepdims=True)
    total = jnp.sum(jnp.exp(scores - top), axis=-1, keepdims=True)
    lse = top + jnp.log(total)
    prob = jnp.exp(scores - lse)
    prob_b = lax.optimization_barrier(prob.astype(jnp.bfloat16)).astype(jnp.float32)
    attn = jnp.einsum("gtw,wd->tgd", prob_b, value_f).astype(jnp.bfloat16)
    attn_f = lax.optimization_barrier(attn).astype(jnp.float32)
    delta = jnp.sum(dout_f * attn_f, axis=-1)
    dprob = jnp.einsum("tgd,wd->gtw", dout_f, value_f)
    dscore = (prob * (dprob - jnp.transpose(delta)[:, :, None]) * scale).astype(jnp.bfloat16)
    dscore_f = lax.optimization_barrier(dscore).astype(jnp.float32)
    grad_q = jnp.einsum("gtw,wd->tgd", dscore_f, key_f).astype(jnp.bfloat16)
    key_gradient = jnp.einsum("gtw,tgd->wd", dscore_f, query_f)
    value_gradient = jnp.einsum("gtw,tgd->wd", prob_b, dout_f)
    return attn, grad_q, key_gradient, value_gradient


def microbatch(parts):
    queries, keys, values, output_cotangent, doc_start = parts
    local_tokens = TOK_DEV
    token_span = (REACH + 1) * local_tokens
    leading_rows = REACH * local_tokens
    scale = HEAD_WIDTH ** -0.5
    paired_rows = jnp.stack([keys, values])
    padded_rows = jnp.concatenate([jnp.zeros((2, leading_rows, KEY_VALUE_HEADS * HEAD_WIDTH), paired_rows.dtype), paired_rows], axis=1)

    def step(accum, block):
        leading_entry = (block * local_tokens).astype(jnp.int32)
        query_matrix = lax.dynamic_slice_in_dim(queries, leading_entry, local_tokens, 0).reshape(local_tokens, KEY_VALUE_HEADS, QUERY_PER_KV, HEAD_WIDTH)
        output_grad_rows = lax.dynamic_slice_in_dim(output_cotangent, leading_entry, local_tokens, 0).reshape(local_tokens, KEY_VALUE_HEADS, QUERY_PER_KV, HEAD_WIDTH)
        starts = lax.dynamic_slice_in_dim(doc_start, leading_entry, local_tokens, 0)
        attention_window = lax.dynamic_slice_in_dim(padded_rows, leading_entry, token_span, 1).reshape(2, token_span, KEY_VALUE_HEADS, HEAD_WIDTH)
        query_pos = leading_entry + jnp.arange(local_tokens, dtype=jnp.int32)
        key_pos = leading_entry - leading_rows + jnp.arange(token_span, dtype=jnp.int32)
        visible = (key_pos[None, :] >= starts[:, None]) & (key_pos[None, :] <= query_pos[:, None])

        def per_group(items):
            return group_terms(items[0], items[1], items[2], items[3], visible, scale)

        attn, grad_q, key_gradient, value_gradient = lax.map(per_group, (jnp.moveaxis(query_matrix, 1, 0), jnp.moveaxis(output_grad_rows, 1, 0), jnp.moveaxis(attention_window[0], 1, 0), jnp.moveaxis(attention_window[1], 1, 0)))
        attn_rows = jnp.moveaxis(attn, 0, 1).reshape(local_tokens, QUERY_HEADS * HEAD_WIDTH)
        grad_q_rows = jnp.moveaxis(grad_q, 0, 1).reshape(local_tokens, QUERY_HEADS * HEAD_WIDTH)
        key_value_gradient = jnp.stack([jnp.moveaxis(key_gradient, 0, 1).reshape(token_span, KEY_VALUE_HEADS * HEAD_WIDTH), jnp.moveaxis(value_gradient, 0, 1).reshape(token_span, KEY_VALUE_HEADS * HEAD_WIDTH)])
        current = lax.dynamic_slice_in_dim(accum, leading_entry, token_span, 1)
        accum = lax.dynamic_update_slice_in_dim(accum, current + key_value_gradient, leading_entry, 1)
        return accum, (attn_rows, grad_q_rows)

    initial_accumulator = jnp.zeros((2, leading_rows + TOKEN_LENGTH, KEY_VALUE_HEADS * HEAD_WIDTH), jnp.float32)
    accum, (attn, grad_q) = lax.scan(step, initial_accumulator, jnp.arange(N_CTX, dtype=jnp.int32))
    return attn.reshape(TOKEN_LENGTH, QUERY_HEADS * HEAD_WIDTH), grad_q.reshape(TOKEN_LENGTH, QUERY_HEADS * HEAD_WIDTH), accum[:, leading_rows:].astype(jnp.bfloat16)


def reference(queries, keys, values, output_cotangent, doc_start):
    attn, grad_q, key_value_gradient = lax.map(microbatch, (queries, keys, values, output_cotangent, doc_start))
    handed_dq = jnp.concatenate([grad_q[1:], jnp.zeros_like(grad_q[:1])], axis=0)
    handed_kv = jnp.concatenate([key_value_gradient[1:], jnp.zeros_like(key_value_gradient[:1])], axis=0)
    return attn, handed_dq, handed_kv
```

```python
import functools

import jax
import jax.numpy as jnp
from jax import lax
from jax.experimental import pallas as pl
from jax.experimental.pallas import tpu as pltpu
from jax.sharding import PartitionSpec as P

WIDTH = 128
REACH = 3
LOG2E = 1.4426950408889634
HIDDEN = -1e30
MESH = pl.DeviceIdType.MESH
NT = (((1,), (1,)), ((), ()))
NN = (((1,), (0,)), ((), ()))
TN = (((0,), (0,)), ((), ()))


def dot(a, b, dims):
    return lax.dot_general(a, b, dims, preferred_element_type=jnp.float32)


def body(
    n, sections, groups, per,
    doc_ref, q_hbm, k_hbm, v_hbm, do_hbm,
    attn_hbm, dq_hbm, kv_hbm,
    win, q_v, do_v, attn_v, dq_v, bias, acc, own, part, xbuf, xin, rbuf, rin, zbuf,
    kvl_sem, ql_sem, al_sem, kv_send, kv_recv, x_send, x_recv, r_send, r_recv,
    dq_send, dq_recv, z_send, z_recv,
):
    tok = q_v.shape[0]
    sec, d = lax.axis_index("section"), lax.axis_index("ctx")
    odd = lax.rem(d, 2) == 1
    even = lax.rem(d, 2) == 0
    mate = d + 1 - 2 * lax.rem(d, 2)
    has = {-1: d >= 1, -3: d >= 3, 1: d + 1 < n, 3: d + 3 < n}
    up, down = sec + 1 < sections, sec >= 1
    scale = WIDTH ** (-0.5)

    def slot(s):
        return pl.ds(s * tok, tok)

    def lanes(i, count=1):
        return pl.ds(pl.multiple_of(i * count * WIDTH, WIDTH), count * WIDTH)

    def load_kv(g, which):
        src = (k_hbm, v_hbm)[which]
        return pltpu.make_async_copy(
            src.at[:, lanes(g)], win.at[g, which, slot(REACH), :], kvl_sem.at[g, which]
        )

    def load_q(g, which):
        src, dst = ((q_hbm, q_v), (do_hbm, do_v))[which]
        return pltpu.make_async_copy(
            src.at[:, lanes(g, per)], dst.at[:, lanes(g, per)], ql_sem.at[g, which]
        )

    def store_attn(g):
        return pltpu.make_async_copy(
            attn_v.at[:, lanes(g, per)], attn_hbm.at[:, lanes(g, per)], al_sem.at[g]
        )

    def kv_copy(g, src_slot, dst_slot, kind, target):
        return pltpu.make_async_remote_copy(
            src_ref=win.at[g, :, slot(src_slot), :],
            dst_ref=win.at[g, :, slot(dst_slot), :],
            send_sem=kv_send.at[g, kind],
            recv_sem=kv_recv.at[g, dst_slot],
            device_id=(sec, target),
            device_id_type=MESH,
        )

    def x_copy(g):
        return pltpu.make_async_remote_copy(
            src_ref=xbuf.at[g], dst_ref=xin.at[g], send_sem=x_send.at[g], recv_sem=x_recv.at[g],
            device_id=(sec, mate), device_id_type=MESH,
        )

    def r_copy(g, i):
        return pltpu.make_async_remote_copy(
            src_ref=rbuf.at[g, i], dst_ref=rin.at[g, i],
            send_sem=r_send.at[g, i], recv_sem=r_recv.at[g, i],
            device_id=(sec, d - (1, 3)[i]), device_id_type=MESH,
        )

    def dq_copy(h):
        return pltpu.make_async_remote_copy(
            src_ref=dq_v.at[h], dst_ref=dq_hbm.at[:, lanes(h)],
            send_sem=dq_send.at[h], recv_sem=dq_recv.at[h],
            device_id=(sec - 1, d), device_id_type=MESH,
        )

    def z_copy(g):
        return pltpu.make_async_remote_copy(
            src_ref=zbuf.at[g], dst_ref=kv_hbm.at[:, :, lanes(g)],
            send_sem=z_send.at[g], recv_sem=z_recv.at[g],
            device_id=(sec - 1, d), device_id_type=MESH,
        )

    def send_own(g):
        load_kv(g, 0).wait()
        load_kv(g, 1).wait()
        pl.when(has[1])(lambda: kv_copy(g, 3, 2, 0, d + 1).start())
        pl.when(has[3])(lambda: kv_copy(g, 3, 0, 1, d + 3).start())

    def forward(g):
        @pl.when(has[-1] & even)
        def _():
            kv_copy(g, 2, 2, 0, d).wait_recv()
            kv_copy(g, 2, 1, 2, mate).start()

        @pl.when(has[-3] & odd)
        def _():
            kv_copy(g, 0, 0, 1, d).wait_recv()
            kv_copy(g, 0, 1, 2, mate).start()

    def arrive(g):
        pl.when(has[-1] & odd)(lambda: kv_copy(g, 2, 2, 0, d).wait_recv())
        pl.when(has[-3] & even)(lambda: kv_copy(g, 0, 0, 1, d).wait_recv())
        pl.when(d >= 2)(lambda: kv_copy(g, 1, 1, 2, d).wait_recv())

    def give(g):
        own[g] = acc[:, slot(3), :]
        part[g, 0] = acc[:, slot(2), :]
        part[g, 1] = acc[:, slot(0), :]
        xbuf[g] = acc[:, slot(1), :].astype(jnp.bfloat16)
        pl.when(d >= 2)(lambda: x_copy(g).start())

    def pass_on(g):
        @pl.when(d >= 2)
        def _():
            x_copy(g).wait_recv()

            @pl.when(even)
            def _():
                part[g, 0] += xin[g].astype(jnp.float32)

            @pl.when(odd)
            def _():
                part[g, 1] += xin[g].astype(jnp.float32)

        @pl.when(has[-1])
        def _():
            rbuf[g, 0] = part[g, 0].astype(jnp.bfloat16)
            r_copy(g, 0).start()

        @pl.when(has[-3])
        def _():
            rbuf[g, 1] = part[g, 1].astype(jnp.bfloat16)
            r_copy(g, 1).start()

    def finish(g):
        @pl.when(has[1])
        def _():
            r_copy(g, 0).wait_recv()
            own[g] += rin[g, 0].astype(jnp.float32)

        @pl.when(has[3])
        def _():
            r_copy(g, 1).wait_recv()
            own[g] += rin[g, 1].astype(jnp.float32)

        zbuf[g] = own[g].astype(jnp.bfloat16)
        pl.when(down)(lambda: z_copy(g).start())

    for g in range(groups):
        load_kv(g, 0).start()
        load_kv(g, 1).start()
        if g == 0:
            load_q(0, 0).start()
            load_q(0, 1).start()
    for g in range(1, groups):
        load_q(g, 0).start()
        load_q(g, 1).start()

    barrier = pltpu.get_barrier_semaphore()

    def greet(there, where):
        @pl.when(there)
        def _():
            pl.semaphore_signal(barrier, inc=1, device_id=where, device_id_type=MESH)

    for off in (-1, 1, -3, 3):
        greet(has[off], (sec, d + off))
    greet(up, (sec + 1, d))
    greet(down, (sec - 1, d))
    peers = sum(x.astype(jnp.int32) for x in (has[-1], has[1], has[-3], has[3], up, down))
    pl.semaphore_wait(barrier, peers)

    send_own(0)

    for s, missing in ((2, d < 1), (1, d < 2), (0, d < 3)):
        @pl.when(missing)
        def _():
            for g in range(groups):
                win[g, :, slot(s), :] = jnp.zeros((2, tok, WIDTH), win.dtype)

    starts = jnp.transpose(jnp.broadcast_to(doc_ref[...], (tok, tok)))
    rows = d * tok + lax.broadcasted_iota(jnp.int32, (tok, tok), 0)
    columns = lax.broadcasted_iota(jnp.int32, (tok, tok), 1)
    for s in range(REACH + 1):
        key_pos = (d - REACH + s) * tok + columns
        seen = (key_pos >= starts) & (key_pos <= rows)
        bias[:, slot(s)] = jnp.where(seen, 0.0, HIDDEN)

    forward(0)

    def head(g, i):
        h = g * per + i
        q, do = q_v[:, lanes(h)], do_v[:, lanes(h)]
        keys, values = win[g, 0], win[g, 1]
        t = dot(q, keys, NT) * (scale * LOG2E) + bias[...]
        top = jnp.max(t, axis=1, keepdims=True)
        p = jnp.exp2(t - top)
        prob = p * (1.0 / jnp.sum(p, axis=1, keepdims=True))
        prob_b = prob.astype(jnp.bfloat16)
        attn = dot(prob_b, values, NN).astype(jnp.bfloat16)
        attn_v[:, lanes(h)] = attn
        delta = jnp.sum(do.astype(jnp.float32) * attn.astype(jnp.float32), axis=1, keepdims=True)
        dprob = dot(do, values, NT)
        ds = (prob * (dprob - delta) * scale).astype(jnp.bfloat16)
        dq_v[h] = dot(ds, keys, NN).astype(jnp.bfloat16)
        pl.when(down)(lambda: dq_copy(h).start())
        gk, gv = dot(ds, q, TN), dot(prob_b, do, TN)
        if i == 0:
            acc[0], acc[1] = gk, gv
        else:
            acc[0] += gk
            acc[1] += gv

    def group(g, _):
        load_q(g, 0).wait()
        load_q(g, 1).wait()
        arrive(g)
        pl.when(g + 1 < groups)(lambda: send_own(g + 1))
        for i in range(per):
            head(g, i)
            if i == 1:
                pl.when(g >= 1)(lambda: pass_on(g - 1))
            if i == 3:
                pl.when(g + 1 < groups)(lambda: forward(g + 1))
        store_attn(g).start()
        give(g)
        pl.when(g >= 1)(lambda: finish(g - 1))
        return 0

    lax.fori_loop(0, groups, group, 0)
    pass_on(groups - 1)
    finish(groups - 1)

    def drain(g, _):
        store_attn(g).wait()
        pl.when(has[1])(lambda: kv_copy(g, 3, 2, 0, d + 1).wait_send())
        pl.when(has[3])(lambda: kv_copy(g, 3, 0, 1, d + 3).wait_send())
        pl.when((has[-1] & even) | (has[-3] & odd))(lambda: kv_copy(g, 2, 1, 2, mate).wait_send())
        pl.when(d >= 2)(lambda: x_copy(g).wait_send())
        pl.when(has[-1])(lambda: r_copy(g, 0).wait_send())
        pl.when(has[-3])(lambda: r_copy(g, 1).wait_send())

        def each(i, _):
            pl.when(down)(lambda: dq_copy(g * per + i).wait_send())
            pl.when(up)(lambda: dq_copy(g * per + i).wait_recv())
            return 0

        lax.fori_loop(0, per, each, 0)
        pl.when(down)(lambda: z_copy(g).wait_send())
        pl.when(up)(lambda: z_copy(g).wait_recv())
        return 0

    lax.fori_loop(0, groups, drain, 0)


def solution(mesh):
    n, sections = mesh.shape["ctx"], mesh.shape["section"]

    def local(queries, keys, values, output_cotangent, doc_start):
        tok, wide = queries.shape[1:]
        narrow = keys.shape[2]
        groups, per = narrow // WIDTH, wide // narrow
        heads = groups * per
        bf, f4 = jnp.bfloat16, jnp.float32
        dma = pltpu.SemaphoreType.DMA
        anywhere = pl.BlockSpec(memory_space=pl.ANY)
        attn, dq, kv = pl.pallas_call(
            functools.partial(body, n, sections, groups, per),
            out_shape=(
                jax.ShapeDtypeStruct((tok, wide), bf),
                jax.ShapeDtypeStruct((tok, wide), bf),
                jax.ShapeDtypeStruct((2, tok, narrow), bf),
            ),
            in_specs=[pl.BlockSpec(memory_space=pltpu.VMEM)] + [anywhere] * 4,
            out_specs=(anywhere,) * 3,
            scratch_shapes=[
                pltpu.VMEM((groups, 2, (REACH + 1) * tok, WIDTH), bf),
                pltpu.VMEM((tok, wide), bf),
                pltpu.VMEM((tok, wide), bf),
                pltpu.VMEM((tok, wide), bf),
                pltpu.VMEM((heads, tok, WIDTH), bf),
                pltpu.VMEM((tok, (REACH + 1) * tok), f4),
                pltpu.VMEM((2, (REACH + 1) * tok, WIDTH), f4),
                pltpu.VMEM((groups, 2, tok, WIDTH), f4),
                pltpu.VMEM((groups, 2, 2, tok, WIDTH), f4),
                pltpu.VMEM((groups, 2, tok, WIDTH), bf),
                pltpu.VMEM((groups, 2, tok, WIDTH), bf),
                pltpu.VMEM((groups, 2, 2, tok, WIDTH), bf),
                pltpu.VMEM((groups, 2, 2, tok, WIDTH), bf),
                pltpu.VMEM((groups, 2, tok, WIDTH), bf),
                dma((groups, 2)), dma((groups, 2)), dma((groups,)),
                dma((groups, 3)), dma((groups, 3)),
                dma((groups,)), dma((groups,)),
                dma((groups, 2)), dma((groups, 2)),
                dma((heads,)), dma((heads,)),
                dma((groups,)), dma((groups,)),
            ],
            compiler_params=pltpu.CompilerParams(
                collective_id=0, has_side_effects=True, vmem_limit_bytes=48 * 2**20
            ),
        )(doc_start, queries[0], keys[0], values[0], output_cotangent[0])
        last = lax.axis_index("section") == sections - 1
        dq = jnp.where(last, jnp.zeros_like(dq), dq)
        kv = jnp.where(last, jnp.zeros_like(kv), kv)
        return attn[None], dq[None], kv[None]

    rows = P("section", "ctx", None)
    return jax.shard_map(
        local,
        mesh=mesh,
        in_specs=(rows, rows, rows, rows, P("section", "ctx")),
        out_specs=(rows, rows, P("section", None, "ctx", None)),
        check_vma=False,
    )
```

```python
import functools

import jax
import jax.numpy as jnp
from jax import lax
from jax.experimental import pallas as pl
from jax.experimental.pallas import tpu as pltpu
from jax.sharding import PartitionSpec as P

WIDTH = 128
REACH = 3
LOG2E = 1.4426950408889634
HIDDEN = -1e30
MESH = pl.DeviceIdType.MESH
NT = (((1,), (1,)), ((), ()))
NN = (((1,), (0,)), ((), ()))
TN = (((0,), (0,)), ((), ()))


def dot(a, b, dims):
    return lax.dot_general(a, b, dims, preferred_element_type=jnp.float32)


def body(
    n, sections, groups, per,
    doc_ref, q_hbm, k_hbm, v_hbm, do_hbm,
    attn_hbm, dq_hbm, kv_hbm,
    win, q_v, do_v, attn_v, dq_v, bias, acc, own, part, xbuf, xin, rbuf, rin, zbuf,
    kvl_sem, ql_sem, al_sem, kv_send, kv_recv, x_send, x_recv, r_send, r_recv,
    dq_send, dq_recv, z_send, z_recv,
):
    tok = q_v.shape[0]
    sec, d = lax.axis_index("section"), lax.axis_index("ctx")
    odd = lax.rem(d, 2) == 1
    even = lax.rem(d, 2) == 0
    mate = d + 1 - 2 * lax.rem(d, 2)
    has = {-1: d >= 1, -3: d >= 3, 1: d + 1 < n, 3: d + 3 < n}
    up, down = sec + 1 < sections, sec >= 1
    scale = WIDTH ** (-0.5)

    def slot(s):
        return pl.ds(s * tok, tok)

    def lanes(i, count=1):
        return pl.ds(pl.multiple_of(i * count * WIDTH, WIDTH), count * WIDTH)

    def load_kv(g, which):
        src = (k_hbm, v_hbm)[which]
        return pltpu.make_async_copy(
            src.at[:, lanes(g)], win.at[g, which, slot(REACH), :], kvl_sem.at[g, which]
        )

    def load_q(g, which):
        src, dst = ((q_hbm, q_v), (do_hbm, do_v))[which]
        return pltpu.make_async_copy(
            src.at[:, lanes(g, per)], dst.at[:, lanes(g, per)], ql_sem.at[g, which]
        )

    def store_attn(g):
        return pltpu.make_async_copy(
            attn_v.at[:, lanes(g, per)], attn_hbm.at[:, lanes(g, per)], al_sem.at[g]
        )

    def kv_copy(g, src_slot, dst_slot, kind, target):
        return pltpu.make_async_remote_copy(
            src_ref=win.at[g, :, slot(src_slot), :],
            dst_ref=win.at[g, :, slot(dst_slot), :],
            send_sem=kv_send.at[g, kind],
            recv_sem=kv_recv.at[g, dst_slot],
            device_id=(sec, target),
            device_id_type=MESH,
        )

    def x_copy(g):
        return pltpu.make_async_remote_copy(
            src_ref=xbuf.at[g], dst_ref=xin.at[g], send_sem=x_send.at[g], recv_sem=x_recv.at[g],
            device_id=(sec, mate), device_id_type=MESH,
        )

    def r_copy(g, i):
        return pltpu.make_async_remote_copy(
            src_ref=rbuf.at[g, i], dst_ref=rin.at[g, i],
            send_sem=r_send.at[g, i], recv_sem=r_recv.at[g, i],
            device_id=(sec, d - (1, 3)[i]), device_id_type=MESH,
        )

    def dq_copy(h):
        return pltpu.make_async_remote_copy(
            src_ref=dq_v.at[h], dst_ref=dq_hbm.at[:, lanes(h)],
            send_sem=dq_send.at[h], recv_sem=dq_recv.at[h],
            device_id=(sec - 1, d), device_id_type=MESH,
        )

    def z_copy(g):
        return pltpu.make_async_remote_copy(
            src_ref=zbuf.at[g], dst_ref=kv_hbm.at[:, :, lanes(g)],
            send_sem=z_send.at[g], recv_sem=z_recv.at[g],
            device_id=(sec - 1, d), device_id_type=MESH,
        )

    def send_own(g):
        load_kv(g, 0).wait()
        load_kv(g, 1).wait()
        pl.when(has[1])(lambda: kv_copy(g, 3, 2, 0, d + 1).start())
        pl.when(has[3])(lambda: kv_copy(g, 3, 0, 1, d + 3).start())

    def forward(g):
        @pl.when(has[-1] & even)
        def _():
            kv_copy(g, 2, 2, 0, d).wait_recv()
            kv_copy(g, 2, 1, 2, mate).start()

        @pl.when(has[-3] & odd)
        def _():
            kv_copy(g, 0, 0, 1, d).wait_recv()
            kv_copy(g, 0, 1, 2, mate).start()

    def arrive(g):
        pl.when(has[-1] & odd)(lambda: kv_copy(g, 2, 2, 0, d).wait_recv())
        pl.when(has[-3] & even)(lambda: kv_copy(g, 0, 0, 1, d).wait_recv())
        pl.when(d >= 2)(lambda: kv_copy(g, 1, 1, 2, d).wait_recv())

    def give(g):
        own[g] = acc[:, slot(3), :]
        part[g, 0] = acc[:, slot(2), :]
        part[g, 1] = acc[:, slot(0), :]
        xbuf[g] = acc[:, slot(1), :].astype(jnp.bfloat16)
        pl.when(d >= 2)(lambda: x_copy(g).start())

    def pass_on(g):
        @pl.when(d >= 2)
        def _():
            x_copy(g).wait_recv()

            @pl.when(even)
            def _():
                part[g, 0] += xin[g].astype(jnp.float32)

            @pl.when(odd)
            def _():
                part[g, 1] += xin[g].astype(jnp.float32)

        @pl.when(has[-1])
        def _():
            rbuf[g, 0] = part[g, 0].astype(jnp.bfloat16)
            r_copy(g, 0).start()

        @pl.when(has[-3])
        def _():
            rbuf[g, 1] = part[g, 1].astype(jnp.bfloat16)
            r_copy(g, 1).start()

    def finish(g):
        @pl.when(has[1])
        def _():
            r_copy(g, 0).wait_recv()
            own[g] += rin[g, 0].astype(jnp.float32)

        @pl.when(has[3])
        def _():
            r_copy(g, 1).wait_recv()
            own[g] += rin[g, 1].astype(jnp.float32)

        zbuf[g] = own[g].astype(jnp.bfloat16)
        pl.when(down)(lambda: z_copy(g).start())

    for g in range(groups):
        load_kv(g, 0).start()
        load_kv(g, 1).start()
        if g == 0:
            load_q(0, 0).start()
            load_q(0, 1).start()
    for g in range(1, groups):
        load_q(g, 0).start()
        load_q(g, 1).start()

    barrier = pltpu.get_barrier_semaphore()

    def greet(there, where):
        @pl.when(there)
        def _():
            pl.semaphore_signal(barrier, inc=1, device_id=where, device_id_type=MESH)

    for off in (-1, 1, -3, 3):
        greet(has[off], (sec, d + off))
    greet(up, (sec + 1, d))
    greet(down, (sec - 1, d))
    peers = sum(x.astype(jnp.int32) for x in (has[-1], has[1], has[-3], has[3], up, down))
    pl.semaphore_wait(barrier, peers)

    send_own(0)

    for s, missing in ((2, d < 1), (1, d < 2), (0, d < 3)):
        @pl.when(missing)
        def _():
            for g in range(groups):
                win[g, :, slot(s), :] = jnp.zeros((2, tok, WIDTH), win.dtype)

    starts = jnp.transpose(jnp.broadcast_to(doc_ref[...], (tok, tok)))
    rows = d * tok + lax.broadcasted_iota(jnp.int32, (tok, tok), 0)
    columns = lax.broadcasted_iota(jnp.int32, (tok, tok), 1)
    for s in range(REACH + 1):
        key_pos = (d - REACH + s) * tok + columns
        seen = (key_pos >= starts) & (key_pos <= rows)
        bias[:, slot(s)] = jnp.where(seen, 0.0, HIDDEN)

    forward(0)

    def head(g, i):
        h = g * per + i
        q, do = q_v[:, lanes(h)], do_v[:, lanes(h)]
        keys, values = win[g, 0], win[g, 1]
        t = dot(q, keys, NT) * (scale * LOG2E) + bias[...]
        top = jnp.max(t, axis=1, keepdims=True)
        p = jnp.exp2(t - top)
        prob = p * (1.0 / jnp.sum(p, axis=1, keepdims=True))
        prob_b = prob.astype(jnp.bfloat16)
        attn = dot(prob_b, values, NN).astype(jnp.bfloat16)
        attn_v[:, lanes(h)] = attn
        delta = jnp.sum(do.astype(jnp.float32) * attn.astype(jnp.float32), axis=1, keepdims=True)
        dprob = dot(do, values, NT)
        ds = (prob * (dprob - delta) * scale).astype(jnp.bfloat16)
        dq_v[h] = dot(ds, keys, NN).astype(jnp.bfloat16)
        pl.when(down)(lambda: dq_copy(h).start())
        gk, gv = dot(ds, q, TN), dot(prob_b, do, TN)
        if i == 0:
            acc[0], acc[1] = gk, gv
        else:
            acc[0] += gk
            acc[1] += gv

    def group(g, _):
        load_q(g, 0).wait()
        load_q(g, 1).wait()
        arrive(g)
        pl.when(g + 1 < groups)(lambda: send_own(g + 1))
        for i in range(per):
            head(g, i)
            if i == 1:
                pl.when(g >= 1)(lambda: pass_on(g - 1))
            if i == 3:
                pl.when(g + 1 < groups)(lambda: forward(g + 1))
        store_attn(g).start()
        give(g)
        pl.when(g >= 1)(lambda: finish(g - 1))
        return 0

    lax.fori_loop(0, groups, group, 0)
    pass_on(groups - 1)
    finish(groups - 1)

    def drain(g, _):
        store_attn(g).wait()
        pl.when(has[1])(lambda: kv_copy(g, 3, 2, 0, d + 1).wait_send())
        pl.when(has[3])(lambda: kv_copy(g, 3, 0, 1, d + 3).wait_send())
        pl.when((has[-1] & even) | (has[-3] & odd))(lambda: kv_copy(g, 2, 1, 2, mate).wait_send())
        pl.when(d >= 2)(lambda: x_copy(g).wait_send())
        pl.when(has[-1])(lambda: r_copy(g, 0).wait_send())
        pl.when(has[-3])(lambda: r_copy(g, 1).wait_send())

        def each(i, _):
            pl.when(down)(lambda: dq_copy(g * per + i).wait_send())
            pl.when(up)(lambda: dq_copy(g * per + i).wait_recv())
            return 0

        lax.fori_loop(0, per, each, 0)
        pl.when(down)(lambda: z_copy(g).wait_send())
        pl.when(up)(lambda: z_copy(g).wait_recv())
        return 0

    lax.fori_loop(0, groups, drain, 0)


def settle(sections, attn_in, dq_in, kv_in, attn_out, dq_out, kv_out, zero, sems):
    last = lax.axis_index("section") == sections - 1
    first = pltpu.make_async_copy(attn_in, attn_out, sems.at[0])
    first.start()
    narrow = kv_in.shape[2]

    @pl.when(last)
    def _():
        zero[...] = jnp.zeros_like(zero)
        copies = [pltpu.make_async_copy(zero, dq_out, sems.at[1])]
        for i in range(2):
            copies.append(
                pltpu.make_async_copy(zero.at[:, pl.ds(0, narrow)], kv_out.at[i], sems.at[2 + i])
            )
        for copy in copies:
            copy.start()
        for copy in copies:
            copy.wait()

    @pl.when(jnp.logical_not(last))
    def _():
        copies = [
            pltpu.make_async_copy(dq_in, dq_out, sems.at[1]),
            pltpu.make_async_copy(kv_in, kv_out, sems.at[2]),
        ]
        for copy in copies:
            copy.start()
        for copy in copies:
            copy.wait()

    first.wait()


def solution(mesh):
    n, sections = mesh.shape["ctx"], mesh.shape["section"]

    def local(queries, keys, values, output_cotangent, doc_start):
        tok, wide = queries.shape[1:]
        narrow = keys.shape[2]
        groups, per = narrow // WIDTH, wide // narrow
        heads = groups * per
        bf, f4 = jnp.bfloat16, jnp.float32
        dma = pltpu.SemaphoreType.DMA
        anywhere = pl.BlockSpec(memory_space=pl.ANY)
        attn, dq, kv = pl.pallas_call(
            functools.partial(body, n, sections, groups, per),
            out_shape=(
                jax.ShapeDtypeStruct((tok, wide), bf),
                jax.ShapeDtypeStruct((tok, wide), bf),
                jax.ShapeDtypeStruct((2, tok, narrow), bf),
            ),
            in_specs=[pl.BlockSpec(memory_space=pltpu.VMEM)] + [anywhere] * 4,
            out_specs=(anywhere,) * 3,
            scratch_shapes=[
                pltpu.VMEM((groups, 2, (REACH + 1) * tok, WIDTH), bf),
                pltpu.VMEM((tok, wide), bf),
                pltpu.VMEM((tok, wide), bf),
                pltpu.VMEM((tok, wide), bf),
                pltpu.VMEM((heads, tok, WIDTH), bf),
                pltpu.VMEM((tok, (REACH + 1) * tok), f4),
                pltpu.VMEM((2, (REACH + 1) * tok, WIDTH), f4),
                pltpu.VMEM((groups, 2, tok, WIDTH), f4),
                pltpu.VMEM((groups, 2, 2, tok, WIDTH), f4),
                pltpu.VMEM((groups, 2, tok, WIDTH), bf),
                pltpu.VMEM((groups, 2, tok, WIDTH), bf),
                pltpu.VMEM((groups, 2, 2, tok, WIDTH), bf),
                pltpu.VMEM((groups, 2, 2, tok, WIDTH), bf),
                pltpu.VMEM((groups, 2, tok, WIDTH), bf),
                dma((groups, 2)), dma((groups, 2)), dma((groups,)),
                dma((groups, 3)), dma((groups, 3)),
                dma((groups,)), dma((groups,)),
                dma((groups, 2)), dma((groups, 2)),
                dma((heads,)), dma((heads,)),
                dma((groups,)), dma((groups,)),
            ],
            compiler_params=pltpu.CompilerParams(
                collective_id=0, has_side_effects=True, vmem_limit_bytes=48 * 2**20
            ),
        )(doc_start, queries[0], keys[0], values[0], output_cotangent[0])
        attn, dq, kv = pl.pallas_call(
            functools.partial(settle, sections),
            out_shape=tuple(jax.ShapeDtypeStruct(x.shape, x.dtype) for x in (attn, dq, kv)),
            in_specs=[anywhere] * 3,
            out_specs=(anywhere,) * 3,
            scratch_shapes=[pltpu.VMEM((tok, wide), bf), dma((4,))],
            compiler_params=pltpu.CompilerParams(vmem_limit_bytes=8 * 2**20),
        )(attn, dq, kv)
        return attn[None], dq[None], kv[None]

    rows = P("section", "ctx", None)
    return jax.shard_map(
        local,
        mesh=mesh,
        in_specs=(rows, rows, rows, rows, P("section", "ctx")),
        out_specs=(rows, rows, P("section", None, "ctx", None)),
        check_vma=False,
    )
```
